256 devices in a mesh: occ: 8 (over x, core), ao: 32 (over y, z).
Axes of the slice: x: 4, y: 4, z: 8, core: 2. Of those that a mesh axis runs over, the one named last changes fastest.
Arguments:
- amplitudes: bfloat16 [4096, 128, 128], P('occ', 'ao'), may hold values from -6 to 6
- blocks: bfloat16 [128, 96, 128, 128], P('ao', 'occ'), may hold values from -0.078125 to 0.078125
- kets: int32 [128, 96], P('ao', 'occ'), may hold values from 0 to 127, as said below
- counts: int32 [128], P('ao'), may hold values from 24 to 96, as said below
Outputs:
- ladder: bfloat16 [4096, 128, 128], P('occ', 'ao')
The draws below stay inside these ranges and needn't reach their ends.
Inputs may be any that keep to these rules, and one draw needn't show every extreme that they name: `kets`: the ket tiles of one bra tile's slots are distinct. `counts`: some bra tile has all 96 slots live.
All inputs are finite; a program needn't handle non-finite values.
Results may differ from the reference program's by a relative error of at most 0.001.
Values may be sent and summed in bfloat16 or wider, within the bound.
No kernel may reach another device: no remote copies, remote signals or barrier semaphores. Data moves between devices by JAX's collectives and lax.ppermute only.
A program may use at most 192 MiB of HBM per device.

```python
import jax
import jax.numpy as jnp
from jax import lax

PT = 128
ROWS = 4096
KT = 128
LIST = 96


def draw_kets(key, part):
    key = jax.random.fold_in(key, 11)
    scores = jax.random.randint(key, (KT, KT), 0, 2 ** 20) * KT + jnp.arange(KT, dtype=jnp.int32)[None, :]
    order = jnp.argsort(scores, axis=1)
    return order[:, :LIST].astype(jnp.int32)


def draw_counts(key, part):
    key = jax.random.fold_in(key, 12)
    values = jax.random.randint(key, (KT,), LIST // 4, LIST + 1)
    return values.at[0].set(LIST).astype(jnp.int32)


def level_of(own_key, extent, cuts, smallest, top_value):
    factor_of = 1.0
    for position, shards_of in cuts:
        steps = jax.random.uniform(jax.random.fold_in(jax.random.fold_in(own_key, 6), position), (shards_of,), jnp.float32, smallest / len(cuts), top_value / len(cuts))
        factor_of = factor_of * jnp.repeat(jnp.exp(steps), extent[position] // shards_of).reshape((-1,) + (1,) * (len(extent) - 1 - position))
    return factor_of


def normal_values(stream_key, shape, width, most, split=(), kind=jnp.bfloat16):
    drawn = jax.random.normal(stream_key, shape, jnp.float32) * width
    if len(split) > 0:
        drawn = level_of(stream_key, shape, split, -0.22, 0.18) * drawn
    return jnp.clip(drawn, min=-most, max=most).astype(kind)


def setup_inputs(seed: int = 0) -> dict:
    seeds = jax.random.split(jax.random.key(seed), 5)
    return {
        "amplitudes": normal_values(seeds[0], (ROWS, KT, PT), 1.0, 6.0, ((0, 8), (1, 32))),
        "blocks": normal_values(seeds[1], (KT, LIST, PT, PT), (PT * LIST // 2) ** -0.5, 0.078125, ((0, 32), (1, 8))),
        "kets": draw_kets(jax.random.fold_in(seeds[4], 71), 0),
        "counts": draw_counts(jax.random.fold_in(seeds[4], 71), 0),
    }


def reference(amplitudes, blocks, kets, counts):
    slots = jnp.arange(LIST, dtype=jnp.int32)

    def one_tile(packed):
        block, ket_row, count = packed
        live = slots < count
        chosen = jnp.take(amplitudes, ket_row, axis=1)
        masked = jnp.where(live[:, None, None], block, jnp.zeros_like(block))
        result = jnp.dot(chosen.reshape(ROWS, LIST * PT), masked.reshape(LIST * PT, PT), preferred_element_type=jnp.float32)
        return result.astype(jnp.bfloat16)

    tiles = lax.map(one_tile, (blocks, kets, counts))
    return jnp.transpose(tiles, (1, 0, 2))
```

```python
import functools

import jax
import jax.numpy as jnp
from jax import lax
from jax.experimental import pallas as pl
from jax.experimental.pallas import tpu as pltpu
from jax.sharding import Mesh, PartitionSpec as P

AXES = ("x", "core", "y", "z")
NX, NC, NY, NZ = 4, 2, 4, 8
TILES, SLOTS, WIDTH = 4, 12, 128
BODY = TILES * SLOTS * WIDTH
VMEM = pl.BlockSpec(memory_space=pltpu.VMEM)
SMEM = pl.BlockSpec(memory_space=pltpu.SMEM)


def near(v):
    return pltpu.with_memory_space_constraint(v, pltpu.VMEM)


def pass_kernel(*refs):
    pass


class Order:
    def __init__(self):
        self.token = jnp.zeros((8, WIDTH), jnp.float32)

    def meet(self, *places):
        values = [near(v) for v in [self.token] + [a[k] for a, k in places]]
        held = pl.pallas_call(
            pass_kernel,
            out_shape=[pltpu.VMEM(v.shape, v.dtype) for v in values],
            in_specs=[VMEM] * len(values),
            out_specs=[VMEM] * len(values),
            input_output_aliases={i: i for i in range(len(values))},
            compiler_params=pltpu.CompilerParams(vmem_limit_bytes=1 << 20),
            cost_estimate=pl.CostEstimate(flops=0, bytes_accessed=0, transcendentals=0),
            name="meet",
        )(*values)
        self.token = held[0]
        for (a, k), value in zip(places, held[1:]):
            a[k] = value


def pack_kernel(first, second, out):
    rows = first.shape[0]

    def one(i, _):
        at = pl.multiple_of(i * 80, 16)
        out[pl.ds(at, 80), :] = first[pl.ds(at, 80), :]
        out[pl.ds(rows + at, 80), :] = second[pl.ds(at, 80), :]
        return 0

    lax.fori_loop(0, rows // 80, one, 0)


def pack(first, second):
    return pl.pallas_call(
        pack_kernel,
        out_shape=pltpu.VMEM((2 * first.shape[0], WIDTH), first.dtype),
        in_specs=[VMEM] * 2,
        out_specs=VMEM,
        compiler_params=pltpu.CompilerParams(vmem_limit_bytes=1 << 20),
        name="pack",
    )(near(first), near(second))


def pairs_of(move):
    pairs = []
    for x in range(NX):
        for c in range(NC):
            for y in range(NY):
                for z in range(NZ):
                    tx, tc, ty, tz = move(x, c, y, z)
                    to = ((tx % NX * NC + tc) * NY + ty) * NZ + tz % NZ
                    pairs.append((((x * NC + c) * NY + y) * NZ + z, to))
    return pairs


ALONG_X = pairs_of(lambda x, c, y, z: (x + 1 - 2 * c, c, y, z))
BACK_X = pairs_of(lambda x, c, y, z: (x - 1 + 2 * c, c, y, z))
ALONG_Z = pairs_of(lambda x, c, y, z: (x, c, y, z + 1 - 2 * c))
BACK_Z = pairs_of(lambda x, c, y, z: (x, c, y, z - 1 + 2 * c))
PARTNER = pairs_of(lambda x, c, y, z: (x, c, y ^ (1 + 2 * c), z))
CROSS = pairs_of(lambda x, c, y, z: (x, c, y ^ (3 - 2 * c), z))
OTHER_CORE = pairs_of(lambda x, c, y, z: (x, 1 - c, y, z))


def send(v, pairs, name):
    with jax.named_scope(name):
        return lax.ppermute(v, AXES, pairs)


def spread_kernel(fresh, steps, counts, *refs):
    dense, listed, kets = refs[-3:]
    shards = [
        ref.at[pl.ds(at, BODY + 16), :] for ref in refs[:-3 if fresh else -4] for at in range(0, ref.shape[0], BODY + 16)
    ]
    x, c, y, z = (lax.axis_index(a) for a in AXES)
    sign = 1 - 2 * c
    for i, shard in enumerate(shards):
        listed[...] = shard[BODY:BODY + 16, :].astype(jnp.float32).astype(jnp.int32)
        pltpu.sync_copy(listed, kets.at[i])
    if fresh:
        def wipe(i, _):
            dense[pl.ds(pl.multiple_of(i * 256, 256), 256), :] = jnp.zeros((256, dense.shape[1]), dense.dtype)
            return 0

        lax.fori_loop(0, dense.shape[0] // 256, wipe, 0)
    for i, (shard, (dx, own)) in enumerate(zip(shards, steps)):
        if own:
            source = ((x - sign * dx) & (NX - 1)) * NC + c
        else:
            source = ((x + sign * dx) & (NX - 1)) * NC + 1 - c

        def one(j, _, i=i, shard=shard, source=source):
            for b in range(TILES):
                k = kets[i, b, j]
                dz = (sign * (z - ((k >> 2) & 7))) & 7
                dy = y ^ (k >> 5)
                kind = jnp.where(dy == 0, 0, jnp.where(dy == 2, 3, jnp.where(dy == 1, 1 + c, 2 - c)))
                p = (dz * 4 + kind) * 4 + (k & 3)

                @pl.when(source * SLOTS + j < counts[b])
                def _():
                    block = shard[pl.ds(pl.multiple_of((b * SLOTS + j) * WIDTH, WIDTH), WIDTH), :]
                    dense[pl.ds(pl.multiple_of(p * WIDTH, WIDTH), WIDTH), b * WIDTH:(b + 1) * WIDTH] = block
            return 0

        lax.fori_loop(0, SLOTS, one, 0)


def spread(counts, shards, steps, dense=None):
    fresh = dense is None
    args = (counts,) + tuple(near(v) for v in tuple(shards) + (() if fresh else (dense,)))
    return pl.pallas_call(
        functools.partial(spread_kernel, fresh, steps),
        out_shape=pltpu.VMEM((NY * NZ * TILES * WIDTH, TILES * WIDTH), jnp.bfloat16),
        in_specs=[SMEM] + [VMEM] * (len(args) - 1),
        out_specs=VMEM,
        scratch_shapes=[pltpu.VMEM((16, WIDTH), jnp.int32), pltpu.SMEM((len(steps), 16, WIDTH), jnp.int32)],
        input_output_aliases={} if fresh else {len(args) - 1: 0},
        compiler_params=pltpu.CompilerParams(vmem_limit_bytes=4 << 20),
        cost_estimate=pl.CostEstimate(flops=0, bytes_accessed=6 << 20, transcendentals=0),
        name="spread",
    )(*args)


def terms_kernel(places, fresh, *refs):
    dense, out = refs[0], refs[-1]
    pieces = refs[1 if fresh else 2:-1]
    acc = None if fresh else refs[1][...]
    for piece, q in zip(pieces, places):
        left = jnp.concatenate([piece[t] for t in range(TILES)], axis=1)
        part = jnp.dot(left, dense[q * 512:(q + 1) * 512, :], preferred_element_type=jnp.float32)
        acc = part if acc is None else acc + part
    out[...] = acc.astype(out.dtype)


def add_terms(dense, total, pieces, dtype=jnp.float32):
    rows = pieces[0][0].shape[1]
    fresh = total is None
    args = (dense,) + (() if fresh else (total,)) + tuple(v for v, _ in pieces)
    return pl.pallas_call(
        functools.partial(terms_kernel, [q for _, q in pieces], fresh),
        out_shape=pltpu.VMEM((rows, TILES * WIDTH), dtype),
        in_specs=[VMEM] * len(args),
        out_specs=VMEM,
        compiler_params=pltpu.CompilerParams(vmem_limit_bytes=6 << 20),
        cost_estimate=pl.CostEstimate(
            flops=2 * rows * 512 * 512 * len(pieces), bytes_accessed=len(pieces) << 20, transcendentals=0
        ),
        name="terms",
    )(*(near(v) for v in args))


def on_device(amplitudes, blocks, kets, counts):
    own = jnp.transpose(amplitudes, (1, 0, 2))
    listed = jnp.pad(kets.astype(jnp.bfloat16), ((0, 16 - TILES), (0, WIDTH - SLOTS)))
    load = jnp.concatenate([blocks.reshape(BODY, WIDTH), listed], axis=0)

    s, q, u, v = {0: own}, {}, {}, {}
    bx, ox, dense = {0: load}, {}, {}
    order = Order()

    def along(a, k, name):
        a[k] = send(a[k - 1], ALONG_Z, name + str(k))

    def cross(a, b, k, name):
        b[k] = send(a[k], CROSS, name + str(k))

    along(s, 1, "s")
    q[0] = send(own, PARTNER, "q0")
    bx[1] = send(load, ALONG_X, "bx1")
    ox[0] = send(load, OTHER_CORE, "ox0")
    cross(s, u, 0, "u")

    order.meet((s, 1), (q, 0), (ox, 0))
    along(s, 2, "s")
    along(q, 1, "q")
    cross(s, u, 1, "u")
    dense[0] = spread(counts, [bx[0], ox[0]], [(0, True), (0, False)])
    order.meet((u, 0))
    cross(q, v, 0, "v")

    order.meet((s, 2), (u, 1), (bx, 1), (dense, 0))
    along(s, 3, "s")
    cross(s, u, 2, "u")
    bx[2] = send(bx[1], ALONG_X, "bx2")
    order.meet((q, 1), (v, 0))
    along(q, 2, "q")
    cross(q, v, 1, "v")
    dense[1] = spread(counts, [bx[1]], [(1, True)], dense[0])

    order.meet((s, 3), (u, 2), (dense, 1))
    along(s, 4, "s")
    cross(s, u, 3, "u")
    order.meet((q, 2), (v, 1))
    along(q, 3, "q")
    cross(q, v, 2, "v")

    order.meet((s, 4), (u, 3), (bx, 2))
    along(s, 5, "s")
    cross(s, u, 4, "u")
    both = pack(bx[1], bx[2])
    ox[1] = send(both, OTHER_CORE, "ox12")
    order.meet((q, 3), (v, 2))
    along(q, 4, "q")
    cross(q, v, 3, "v")
    dense[2] = spread(counts, [bx[2]], [(2, True)], dense[1])

    order.meet((s, 5), (u, 4), (ox, 1), (dense, 2))
    along(s, 6, "s")
    cross(s, u, 5, "u")
    bx[3] = send(bx[2], ALONG_X, "bx3")
    order.meet((q, 4), (v, 3))
    along(q, 5, "q")
    cross(q, v, 4, "v")
    dense[3] = spread(counts, [ox[1]], [(1, False), (2, False)], dense[2])

    order.meet((s, 6), (u, 5), (dense, 3))
    along(s, 7, "s")
    cross(s, u, 6, "u")
    order.meet((q, 5), (v, 4))
    along(q, 6, "q")
    cross(q, v, 5, "v")

    order.meet((s, 7), (u, 6), (bx, 3))
    cross(s, u, 7, "u")
    q[7] = send(q[0], BACK_Z, "q7")
    ox[3] = send(bx[3], OTHER_CORE, "ox3")
    dense[4] = spread(counts, [bx[3]], [(3, True)], dense[3])
    order.meet((q, 6), (v, 5), (dense, 4))
    cross(q, v, 6, "v")

    order.meet((u, 7), (q, 7), (ox, 3))
    cross(q, v, 7, "v")
    dense = spread(counts, [ox[3]], [(3, False)], dense[4])

    def terms(ks, names):
        return [(a[k], k * 4 + i) for k in ks for i, a in enumerate((s, q, u, v)) if "squv"[i] in names]

    total = add_terms(dense, None, terms(range(0, 3), "squv"))
    total = add_terms(dense, total, terms(range(3, 6), "squv"))
    total = add_terms(dense, total, terms((6,), "squv") + terms((7,), "squ"))
    out = add_terms(dense, total, terms((7,), "v"), jnp.bfloat16)
    return out.reshape(out.shape[0], TILES, WIDTH)


def solution(mesh):
    grid = Mesh(mesh.devices.reshape(NX, NC, NY, NZ), AXES)
    placed = (
        P(("x", "core"), ("y", "z"), None),
        P(("y", "z"), ("x", "core"), None, None),
        P(("y", "z"), ("x", "core")),
        P(("y", "z")),
    )
    return jax.shard_map(
        on_device, mesh=grid, in_specs=placed, out_specs=P(("x", "core"), ("y", "z"), None), check_vma=False
    )
```

```python
import functools

import jax
import jax.numpy as jnp
from jax import lax
from jax.experimental import pallas as pl
from jax.experimental.pallas import tpu as pltpu
from jax.sharding import Mesh, PartitionSpec as P

AXES = ("x", "core", "y", "z")
NX, NC, NY, NZ = 4, 2, 4, 8
TILES, SLOTS, WIDTH = 4, 12, 128
BODY = TILES * SLOTS * WIDTH
VMEM = pl.BlockSpec(memory_space=pltpu.VMEM)
SMEM = pl.BlockSpec(memory_space=pltpu.SMEM)
ANY = pl.BlockSpec(memory_space=pl.ANY)


def near(v):
    return pltpu.with_memory_space_constraint(v, pltpu.VMEM)


def pass_kernel(*refs):
    pass


class Order:
    def __init__(self):
        self.token = jnp.zeros((8, WIDTH), jnp.float32)

    def meet(self, *places):
        values = [self.token] + [a[k] for a, k in places]
        held = pl.pallas_call(
            pass_kernel,
            out_shape=[jax.ShapeDtypeStruct(v.shape, v.dtype) for v in values],
            in_specs=[ANY] * len(values),
            out_specs=[ANY] * len(values),
            input_output_aliases={i: i for i in range(len(values))},
            compiler_params=pltpu.CompilerParams(vmem_limit_bytes=1 << 20),
            cost_estimate=pl.CostEstimate(flops=0, bytes_accessed=0, transcendentals=0),
            name="meet",
        )(*values)
        self.token = held[0]
        for (a, k), value in zip(places, held[1:]):
            a[k] = value


def pairs_of(move):
    pairs = []
    for x in range(NX):
        for c in range(NC):
            for y in range(NY):
                for z in range(NZ):
                    tx, tc, ty, tz = move(x, c, y, z)
                    to = ((tx % NX * NC + tc) * NY + ty) * NZ + tz % NZ
                    pairs.append((((x * NC + c) * NY + y) * NZ + z, to))
    return pairs


ALONG_X = pairs_of(lambda x, c, y, z: (x + 1 - 2 * c, c, y, z))
BACK_X = pairs_of(lambda x, c, y, z: (x - 1 + 2 * c, c, y, z))
ALONG_Z = pairs_of(lambda x, c, y, z: (x, c, y, z + 1 - 2 * c))
BACK_Z = pairs_of(lambda x, c, y, z: (x, c, y, z - 1 + 2 * c))
PARTNER = pairs_of(lambda x, c, y, z: (x, c, y ^ (1 + 2 * c), z))
CROSS = pairs_of(lambda x, c, y, z: (x, c, y ^ (3 - 2 * c), z))
OTHER_CORE = pairs_of(lambda x, c, y, z: (x, 1 - c, y, z))


def send(v, pairs, name):
    with jax.named_scope(name):
        return lax.ppermute(v, AXES, pairs)


def load_kernel(blocks, kets, out, codes, sems):
    body = pltpu.make_async_copy(blocks, out.at[pl.ds(0, BODY), :], sems.at[0])
    body.start()
    codes[...] = jnp.zeros(codes.shape, codes.dtype)
    codes[0:TILES, 0:SLOTS] = kets[...].astype(jnp.float32)
    half = codes[...].astype(jnp.bfloat16)
    pl.run_scoped(functools.partial(put_codes, half, out, sems), pltpu.VMEM((16, WIDTH), jnp.bfloat16))
    body.wait()


def put_codes(half, out, sems, narrow):
    narrow[...] = half
    tail = pltpu.make_async_copy(narrow, out.at[pl.ds(BODY, 16), :], sems.at[1])
    tail.start()
    tail.wait()


def make_load(blocks, kets):
    return pl.pallas_call(
        load_kernel,
        out_shape=pltpu.HBM((BODY + 16, WIDTH), jnp.bfloat16),
        in_specs=[VMEM, VMEM],
        out_specs=pl.BlockSpec(memory_space=pltpu.HBM),
        scratch_shapes=[pltpu.VMEM((16, WIDTH), jnp.float32), pltpu.SemaphoreType.DMA((2,))],
        compiler_params=pltpu.CompilerParams(vmem_limit_bytes=1 << 20),
        cost_estimate=pl.CostEstimate(flops=0, bytes_accessed=0, transcendentals=0),
        name="load",
    )(near(blocks.reshape(BODY, WIDTH)), kets)


def spread_kernel(tiles, counts, loads, dense, held, codes, listed, kets, sems):
    c, y, z = (lax.axis_index(a) for a in AXES[1:])
    sign = 1 - 2 * c
    rows, span = BODY + 16, SLOTS * WIDTH
    shards = loads.shape[0] // rows
    spare = dense.shape[0] // WIDTH - 1

    code_moves, block_moves = [], []
    for i in range(shards):
        code_moves.append(pltpu.make_async_copy(loads.at[pl.ds(i * rows + BODY, 16), :], codes.at[i], sems.at[i]))
        here = loads.at[pl.ds(i * rows + tiles[0] * span, len(tiles) * span), :]
        block_moves.append(pltpu.make_async_copy(here, held.at[i], sems.at[shards + i]))
    for move in code_moves + block_moves:
        move.start()

    def wipe(i, _):
        dense[pl.ds(pl.multiple_of(i * 512, 512), 512), :] = jnp.zeros((512, dense.shape[1]), dense.dtype)
        return 0

    lax.fori_loop(0, dense.shape[0] // 512, wipe, 0)
    for move in code_moves:
        move.wait()
    for i in range(shards):
        listed[i * 16:(i + 1) * 16, :] = codes[i].astype(jnp.float32).astype(jnp.int32)
    last = pltpu.make_async_copy(listed, kets, sems.at[2 * shards])
    last.start()
    last.wait()
    limits = [counts[t] for t in tiles]

    def place(i, n, j):
        k = kets[i * 16 + tiles[n], j]
        dz = (sign * (z - ((k >> 2) & 7))) & 7
        dy = y ^ (k >> 5)
        kind = jnp.where(dy == 0, 0, jnp.where(dy == 2, 3, jnp.where(dy == 1, 1 + c, 2 - c)))
        return jnp.where(i * SLOTS + j < limits[n], (dz * 4 + kind) * 4 + (k & 3), spare)

    for i in range(shards):
        block_moves[i].wait()

        def some(g, _, i=i):
            picks = [(n, g * 2 + d) for n in range(len(tiles)) for d in range(2)]
            spots = [place(i, n, j) for n, j in picks]
            blocks = [held[i, pl.ds(pl.multiple_of((n * SLOTS + j) * WIDTH, WIDTH), WIDTH), :] for n, j in picks]
            for (n, _), p, block in zip(picks, spots, blocks):
                dense[pl.ds(pl.multiple_of(p * WIDTH, WIDTH), WIDTH), n * WIDTH:(n + 1) * WIDTH] = block
            return 0

        lax.fori_loop(0, SLOTS // 2, some, 0, unroll=True)


def spread(counts, loads, tiles):
    shards = NX * NC
    return pl.pallas_call(
        functools.partial(spread_kernel, tiles),
        out_shape=pltpu.VMEM((NY * NZ * TILES * WIDTH + 512, len(tiles) * WIDTH), jnp.bfloat16),
        in_specs=[SMEM, pl.BlockSpec(memory_space=pltpu.HBM)],
        out_specs=VMEM,
        scratch_shapes=[
            pltpu.VMEM((shards, len(tiles) * SLOTS * WIDTH, WIDTH), jnp.bfloat16),
            pltpu.VMEM((shards, 16, WIDTH), jnp.bfloat16),
            pltpu.VMEM((shards * 16, WIDTH), jnp.int32),
            pltpu.SMEM((shards * 16, WIDTH), jnp.int32),
            pltpu.SemaphoreType.DMA((2 * shards + 1,)),
        ],
        compiler_params=pltpu.CompilerParams(vmem_limit_bytes=10 << 20),
        cost_estimate=pl.CostEstimate(flops=0, bytes_accessed=0, transcendentals=0),
        name="spread",
    )(counts, pltpu.with_memory_space_constraint(loads, pltpu.HBM))


def terms_kernel(places, fresh, *refs):
    dense, out = refs[:2], refs[-1]
    pieces = refs[2 if fresh else 3:-1]
    acc = None if fresh else refs[2][...]
    for piece, q in zip(pieces, places):
        left = jnp.concatenate([piece[t] for t in range(TILES)], axis=1)
        right = jnp.concatenate([d[q * 512:(q + 1) * 512, :] for d in dense], axis=1)
        part = jnp.dot(left, right, preferred_element_type=jnp.float32)
        acc = part if acc is None else acc + part
    out[...] = acc.astype(out.dtype)


def add_terms(dense, total, pieces, dtype=jnp.float32):
    rows = pieces[0][0].shape[1]
    fresh = total is None
    args = (dense[0], dense[1]) + (() if fresh else (total,)) + tuple(v for v, _ in pieces)
    return pl.pallas_call(
        functools.partial(terms_kernel, [q for _, q in pieces], fresh),
        out_shape=pltpu.VMEM((rows, TILES * WIDTH), dtype),
        in_specs=[VMEM] * len(args),
        out_specs=VMEM,
        compiler_params=pltpu.CompilerParams(vmem_limit_bytes=8 << 20),
        cost_estimate=pl.CostEstimate(flops=0, bytes_accessed=0, transcendentals=0),
        name="terms",
    )(*(near(v) for v in args))


def on_device(amplitudes, blocks, kets, counts):
    own = jnp.transpose(amplitudes, (1, 0, 2))
    load = make_load(blocks, kets)

    s, q, u, v = {0: own}, {}, {}, {}
    with jax.named_scope("loads"):
        everything = lax.all_gather(load, ("x", "core"), axis=0, tiled=True)
    order = Order()

    def along(a, k, name):
        a[k] = send(a[k - 1], ALONG_Z, name + str(k))

    def cross(a, b, k, name):
        b[k] = send(a[k], CROSS, name + str(k))

    def turn(k, more_s=(), more_u=(), more_q=(), more_v=()):
        order.meet((s, k), *more_s)
        if k + 1 < NZ:
            along(s, k + 1, "s")
        order.meet((u, k - 1), *more_u)
        cross(s, u, k, "u")
        order.meet((q, k - 1), *more_q)
        if k < NZ - 1:
            along(q, k, "q")
        order.meet((v, k - 2), *more_v)
        cross(q, v, k - 1, "v")

    along(s, 1, "s")
    q[0] = send(own, PARTNER, "q0")
    cross(s, u, 0, "u")
    s[7] = send(own, BACK_Z, "s7")
    order.meet((s, 1))
    along(s, 2, "s")
    cross(s, u, 1, "u")
    order.meet((q, 0))
    along(q, 1, "q")
    cross(q, v, 0, "v")
    order.meet((u, 0))
    order.meet((s, 7))
    for k in range(2, 6):
        turn(k)
    dense = {0: spread(counts, everything, (0, 1))}
    order.meet((s, 6), (dense, 0), (v, 0))
    cross(s, u, 6, "u")
    v[7] = send(v[0], BACK_Z, "v7")
    dense[1] = spread(counts, everything, (2, 3))
    order.meet((u, 5), (q, 5), (dense, 1))
    along(q, 6, "q")
    cross(q, v, 5, "v")

    def terms(ks, names):
        return [(a[k], k * 4 + i) for k in ks for i, a in enumerate((s, q, u, v)) if "squv"[i] in names]

    total = {0: add_terms(dense, None, terms(range(0, 3), "squv"))}
    order.meet((v, 4), (u, 6), (total, 0), (s, 7), (q, 0))
    cross(s, u, 7, "u")
    q[7] = send(q[0], BACK_Z, "q7")
    total[1] = add_terms(dense, total[0], terms((3,), "squv") + terms((4,), "squv") + terms((5,), "squ"))
    order.meet((q, 6), (v, 5), (total, 1))
    cross(q, v, 6, "v")
    total = add_terms(dense, total[1], terms((5,), "v") + terms((6,), "squ") + terms((7,), "suv"))
    out = add_terms(dense, total, terms((7,), "q") + terms((6,), "v"), jnp.bfloat16)
    return out.reshape(out.shape[0], TILES, WIDTH)


def solution(mesh):
    grid = Mesh(mesh.devices.reshape(NX, NC, NY, NZ), AXES)
    placed = (
        P(("x", "core"), ("y", "z"), None),
        P(("y", "z"), ("x", "core"), None, None),
        P(("y", "z"), ("x", "core")),
        P(("y", "z")),
    )
    return jax.shard_map(
        on_device, mesh=grid, in_specs=placed, out_specs=P(("x", "core"), ("y", "z"), None), check_vma=False
    )
```

```python
import functools

import jax
import jax.numpy as jnp
from jax import lax
from jax.experimental import pallas as pl
from jax.experimental.pallas import tpu as pltpu
from jax.sharding import Mesh, PartitionSpec as P

AXES = ("x", "core", "y", "z")
NX, NC, NY, NZ = 4, 2, 4, 8
TILES, SLOTS, WIDTH = 4, 12, 128
BODY = TILES * SLOTS * WIDTH
VMEM = pl.BlockSpec(memory_space=pltpu.VMEM)
SMEM = pl.BlockSpec(memory_space=pltpu.SMEM)
ANY = pl.BlockSpec(memory_space=pl.ANY)


def near(v):
    return pltpu.with_memory_space_constraint(v, pltpu.VMEM)


def pass_kernel(*refs):
    pass


class Order:
    def __init__(self):
        self.token = jnp.zeros((8, WIDTH), jnp.float32)

    def meet(self, *places):
        values = [self.token] + [a[k] for a, k in places]
        held = pl.pallas_call(
            pass_kernel,
            out_shape=[jax.ShapeDtypeStruct(v.shape, v.dtype) for v in values],
            in_specs=[ANY] * len(values),
            out_specs=[ANY] * len(values),
            input_output_aliases={i: i for i in range(len(values))},
            compiler_params=pltpu.CompilerParams(vmem_limit_bytes=1 << 20),
            cost_estimate=pl.CostEstimate(flops=0, bytes_accessed=0, transcendentals=0),
            name="meet",
        )(*values)
        self.token = held[0]
        for (a, k), value in zip(places, held[1:]):
            a[k] = value


def pairs_of(move):
    pairs = []
    for x in range(NX):
        for c in range(NC):
            for y in range(NY):
                for z in range(NZ):
                    tx, tc, ty, tz = move(x, c, y, z)
                    to = ((tx % NX * NC + tc) * NY + ty) * NZ + tz % NZ
                    pairs.append((((x * NC + c) * NY + y) * NZ + z, to))
    return pairs


ALONG_X = pairs_of(lambda x, c, y, z: (x + 1 - 2 * c, c, y, z))
BACK_X = pairs_of(lambda x, c, y, z: (x - 1 + 2 * c, c, y, z))
ALONG_Z = pairs_of(lambda x, c, y, z: (x, c, y, z + 1 - 2 * c))
BACK_Z = pairs_of(lambda x, c, y, z: (x, c, y, z - 1 + 2 * c))
PARTNER = pairs_of(lambda x, c, y, z: (x, c, y ^ (1 + 2 * c), z))
CROSS = pairs_of(lambda x, c, y, z: (x, c, y ^ (3 - 2 * c), z))
OTHER_CORE = pairs_of(lambda x, c, y, z: (x, 1 - c, y, z))


def send(v, pairs, name):
    with jax.named_scope(name):
        return lax.ppermute(v, AXES, pairs)


def load_kernel(blocks, kets, out, codes, sems):
    body = pltpu.make_async_copy(blocks, out.at[pl.ds(0, BODY), :], sems.at[0])
    body.start()
    codes[...] = jnp.zeros(codes.shape, codes.dtype)
    codes[0:TILES, 0:SLOTS] = kets[...].astype(jnp.float32)
    half = codes[...].astype(jnp.bfloat16)
    pl.run_scoped(functools.partial(put_codes, half, out, sems), pltpu.VMEM((16, WIDTH), jnp.bfloat16))
    body.wait()


def put_codes(half, out, sems, narrow):
    narrow[...] = half
    tail = pltpu.make_async_copy(narrow, out.at[pl.ds(BODY, 16), :], sems.at[1])
    tail.start()
    tail.wait()


def make_load(blocks, kets):
    return pl.pallas_call(
        load_kernel,
        out_shape=pltpu.HBM((BODY + 16, WIDTH), jnp.bfloat16),
        in_specs=[VMEM, VMEM],
        out_specs=pl.BlockSpec(memory_space=pltpu.HBM),
        scratch_shapes=[pltpu.VMEM((16, WIDTH), jnp.float32), pltpu.SemaphoreType.DMA((2,))],
        compiler_params=pltpu.CompilerParams(vmem_limit_bytes=1 << 20),
        cost_estimate=pl.CostEstimate(flops=0, bytes_accessed=0, transcendentals=0),
        name="load",
    )(near(blocks.reshape(BODY, WIDTH)), kets)


def spread_kernel(tiles, counts, loads, dense, held, codes, listed, kets, sems):
    c, y, z = (lax.axis_index(a) for a in AXES[1:])
    sign = 1 - 2 * c
    rows, span = BODY + 16, SLOTS * WIDTH
    shards = loads.shape[0] // rows
    spare = dense.shape[0] // WIDTH - 1

    code_moves, block_moves = [], []
    for i in range(shards):
        code_moves.append(pltpu.make_async_copy(loads.at[pl.ds(i * rows + BODY, 16), :], codes.at[i], sems.at[i]))
        here = loads.at[pl.ds(i * rows + tiles[0] * span, len(tiles) * span), :]
        block_moves.append(pltpu.make_async_copy(here, held.at[i], sems.at[shards + i]))
    for move in code_moves + block_moves:
        move.start()

    def wipe(i, _):
        dense[pl.ds(pl.multiple_of(i * 512, 512), 512), :] = jnp.zeros((512, dense.shape[1]), dense.dtype)
        return 0

    lax.fori_loop(0, dense.shape[0] // 512, wipe, 0)
    for move in code_moves:
        move.wait()
    for i in range(shards):
        listed[i * 16:(i + 1) * 16, :] = codes[i].astype(jnp.float32).astype(jnp.int32)
    last = pltpu.make_async_copy(listed, kets, sems.at[2 * shards])
    last.start()
    last.wait()
    limits = [counts[t] for t in tiles]

    def place(i, n, j):
        k = kets[i * 16 + tiles[n], j]
        dz = (sign * (z - ((k >> 2) & 7))) & 7
        dy = y ^ (k >> 5)
        kind = jnp.where(dy == 0, 0, jnp.where(dy == 2, 3, jnp.where(dy == 1, 1 + c, 2 - c)))
        return jnp.where(i * SLOTS + j < limits[n], (dz * 4 + kind) * 4 + (k & 3), spare)

    for i in range(shards):
        block_moves[i].wait()

        def some(g, _, i=i):
            picks = [(n, g * 2 + d) for n in range(len(tiles)) for d in range(2)]
            spots = [place(i, n, j) for n, j in picks]
            blocks = [held[i, pl.ds(pl.multiple_of((n * SLOTS + j) * WIDTH, WIDTH), WIDTH), :] for n, j in picks]
            for (n, _), p, block in zip(picks, spots, blocks):
                dense[pl.ds(pl.multiple_of(p * WIDTH, WIDTH), WIDTH), n * WIDTH:(n + 1) * WIDTH] = block
            return 0

        lax.fori_loop(0, SLOTS // 2, some, 0, unroll=True)


def spread(counts, loads, tiles):
    shards = NX * NC
    return pl.pallas_call(
        functools.partial(spread_kernel, tiles),
        out_shape=pltpu.VMEM((NY * NZ * TILES * WIDTH + 512, len(tiles) * WIDTH), jnp.bfloat16),
        in_specs=[SMEM, pl.BlockSpec(memory_space=pltpu.HBM)],
        out_specs=VMEM,
        scratch_shapes=[
            pltpu.VMEM((shards, len(tiles) * SLOTS * WIDTH, WIDTH), jnp.bfloat16),
            pltpu.VMEM((shards, 16, WIDTH), jnp.bfloat16),
            pltpu.VMEM((shards * 16, WIDTH), jnp.int32),
            pltpu.SMEM((shards * 16, WIDTH), jnp.int32),
            pltpu.SemaphoreType.DMA((2 * shards + 1,)),
        ],
        compiler_params=pltpu.CompilerParams(vmem_limit_bytes=10 << 20),
        cost_estimate=pl.CostEstimate(flops=0, bytes_accessed=0, transcendentals=0),
        name="spread",
    )(counts, pltpu.with_memory_space_constraint(loads, pltpu.HBM))


def terms_kernel(places, fresh, *refs):
    dense, out = refs[:2], refs[-1]
    pieces = refs[2 if fresh else 3:-1]
    acc = None if fresh else refs[2][...]
    for piece, q in zip(pieces, places):
        left = jnp.concatenate([piece[t] for t in range(TILES)], axis=1)
        right = jnp.concatenate([d[q * 512:(q + 1) * 512, :] for d in dense], axis=1)
        part = jnp.dot(left, right, preferred_element_type=jnp.float32)
        acc = part if acc is None else acc + part
    out[...] = acc.astype(out.dtype)


def add_terms(dense, total, pieces, dtype=jnp.float32):
    rows = pieces[0][0].shape[1]
    fresh = total is None
    args = (dense[0], dense[1]) + (() if fresh else (total,)) + tuple(v for v, _ in pieces)
    return pl.pallas_call(
        functools.partial(terms_kernel, [q for _, q in pieces], fresh),
        out_shape=pltpu.VMEM((rows, TILES * WIDTH), dtype),
        in_specs=[VMEM] * len(args),
        out_specs=VMEM,
        compiler_params=pltpu.CompilerParams(vmem_limit_bytes=8 << 20),
        cost_estimate=pl.CostEstimate(flops=0, bytes_accessed=0, transcendentals=0),
        name="terms",
    )(*(near(v) for v in args))


def on_device(amplitudes, blocks, kets, counts):
    own = jnp.transpose(amplitudes, (1, 0, 2))
    load = make_load(blocks, kets)

    s, q, u, v = {0: own}, {}, {}, {}
    with jax.named_scope("loads"):
        everything = lax.all_gather(load, ("x", "core"), axis=0, tiled=True)
    order = Order()

    def along(a, k, name):
        a[k] = send(a[k - 1], ALONG_Z, name + str(k))

    def cross(a, b, k, name):
        b[k] = send(a[k], CROSS, name + str(k))

    def turn(k, more_s=(), more_u=(), more_q=(), more_v=()):
        order.meet((s, k), *more_s)
        if k + 1 < NZ:
            along(s, k + 1, "s")
        order.meet((u, k - 1), *more_u)
        cross(s, u, k, "u")
        order.meet((q, k - 1), *more_q)
        if k < NZ - 1:
            along(q, k, "q")
        order.meet((v, k - 2), *more_v)
        cross(q, v, k - 1, "v")

    along(s, 1, "s")
    q[0] = send(own, PARTNER, "q0")
    cross(s, u, 0, "u")
    s[7] = send(own, BACK_Z, "s7")
    order.meet((s, 1))
    along(s, 2, "s")
    cross(s, u, 1, "u")
    order.meet((q, 0))
    along(q, 1, "q")
    cross(q, v, 0, "v")
    order.meet((u, 0))
    order.meet((s, 7))
    for k in range(2, 6):
        turn(k)
    dense = {0: spread(counts, everything, (0, 1))}
    order.meet((s, 6), (dense, 0))
    cross(s, u, 6, "u")
    order.meet((u, 5))
    order.meet((q, 5))
    along(q, 6, "q")
    cross(q, v, 5, "v")
    dense[1] = spread(counts, everything, (2, 3))

    def terms(ks, names):
        return [(a[k], k * 4 + i) for k in ks for i, a in enumerate((s, q, u, v)) if "squv"[i] in names]

    total = {0: add_terms(dense, None, terms(range(0, 3), "squv"))}
    order.meet((v, 4), (u, 6), (total, 0), (s, 7), (v, 0), (q, 0))
    cross(s, u, 7, "u")
    q[7] = send(q[0], BACK_Z, "q7")
    v[7] = send(v[0], BACK_Z, "v7")
    order.meet((q, 6), (v, 5))
    cross(q, v, 6, "v")
    total[1] = add_terms(dense, total[0], terms((3,), "squv") + terms((4,), "squv") + terms((5,), "squ"))
    total = add_terms(dense, total[1], terms((5,), "v") + terms((6,), "squ") + terms((7,), "suv"))
    out = add_terms(dense, total, terms((7,), "q") + terms((6,), "v"), jnp.bfloat16)
    return out.reshape(out.shape[0], TILES, WIDTH)


def solution(mesh):
    grid = Mesh(mesh.devices.reshape(NX, NC, NY, NZ), AXES)
    placed = (
        P(("x", "core"), ("y", "z"), None),
        P(("y", "z"), ("x", "core"), None, None),
        P(("y", "z"), ("x", "core")),
        P(("y", "z")),
    )
    return jax.shard_map(
        on_device, mesh=grid, in_specs=placed, out_specs=P(("x", "core"), ("y", "z"), None), check_vma=False
    )
```

```python
import functools

import jax
import jax.numpy as jnp
from jax import lax
from jax.experimental import pallas as pl
from jax.experimental.pallas import tpu as pltpu
from jax.sharding import Mesh, PartitionSpec as P

AXES = ("x", "core", "y", "z")
NX, NC, NY, NZ = 4, 2, 4, 8
TILES, SLOTS, WIDTH = 4, 12, 128
BODY = TILES * SLOTS * WIDTH
VMEM = pl.BlockSpec(memory_space=pltpu.VMEM)
SMEM = pl.BlockSpec(memory_space=pltpu.SMEM)
ANY = pl.BlockSpec(memory_space=pl.ANY)


def near(v):
    return pltpu.with_memory_space_constraint(v, pltpu.VMEM)


def pass_kernel(*refs):
    pass


class Order:
    def __init__(self):
        self.token = jnp.zeros((8, WIDTH), jnp.float32)

    def meet(self, *places):
        values = [self.token] + [a[k] for a, k in places]
        held = pl.pallas_call(
            pass_kernel,
            out_shape=[jax.ShapeDtypeStruct(v.shape, v.dtype) for v in values],
            in_specs=[ANY] * len(values),
            out_specs=[ANY] * len(values),
            input_output_aliases={i: i for i in range(len(values))},
            compiler_params=pltpu.CompilerParams(vmem_limit_bytes=1 << 20),
            cost_estimate=pl.CostEstimate(flops=0, bytes_accessed=0, transcendentals=0),
            name="meet",
        )(*values)
        self.token = held[0]
        for (a, k), value in zip(places, held[1:]):
            a[k] = value


def pairs_of(move):
    pairs = []
    for x in range(NX):
        for c in range(NC):
            for y in range(NY):
                for z in range(NZ):
                    tx, tc, ty, tz = move(x, c, y, z)
                    to = ((tx % NX * NC + tc) * NY + ty) * NZ + tz % NZ
                    pairs.append((((x * NC + c) * NY + y) * NZ + z, to))
    return pairs


ALONG_X = pairs_of(lambda x, c, y, z: (x + 1 - 2 * c, c, y, z))
BACK_X = pairs_of(lambda x, c, y, z: (x - 1 + 2 * c, c, y, z))
ALONG_Z = pairs_of(lambda x, c, y, z: (x, c, y, z + 1 - 2 * c))
BACK_Z = pairs_of(lambda x, c, y, z: (x, c, y, z - 1 + 2 * c))
PARTNER = pairs_of(lambda x, c, y, z: (x, c, y ^ (1 + 2 * c), z))
CROSS = pairs_of(lambda x, c, y, z: (x, c, y ^ (3 - 2 * c), z))
OTHER_CORE = pairs_of(lambda x, c, y, z: (x, 1 - c, y, z))


def send(v, pairs, name):
    with jax.named_scope(name):
        return lax.ppermute(v, AXES, pairs)


def load_kernel(blocks, kets, out, codes, held, sems):
    part = BODY // 4
    spans = [pl.ds(i * part, part) for i in range(4)]
    reads = [pltpu.make_async_copy(blocks.at[d, :], held.at[d, :], sems.at[2 + i]) for i, d in enumerate(spans)]
    writes = [pltpu.make_async_copy(held.at[d, :], out.at[d, :], sems.at[6 + i]) for i, d in enumerate(spans)]
    for move in reads:
        move.start()
    for read, write in zip(reads, writes):
        read.wait()
        write.start()
    codes[...] = jnp.zeros(codes.shape, codes.dtype)
    codes[0:TILES, 0:SLOTS] = kets[...].astype(jnp.float32)
    half = codes[...].astype(jnp.bfloat16)
    pl.run_scoped(functools.partial(put_codes, half, out, sems), pltpu.VMEM((16, WIDTH), jnp.bfloat16))
    for move in writes:
        move.wait()


def put_codes(half, out, sems, narrow):
    narrow[...] = half
    tail = pltpu.make_async_copy(narrow, out.at[pl.ds(BODY, 16), :], sems.at[1])
    tail.start()
    tail.wait()


def make_load(blocks, kets):
    return pl.pallas_call(
        load_kernel,
        out_shape=pltpu.HBM((BODY + 16, WIDTH), jnp.bfloat16),
        in_specs=[pl.BlockSpec(memory_space=pltpu.HBM), VMEM],
        out_specs=pl.BlockSpec(memory_space=pltpu.HBM),
        scratch_shapes=[
            pltpu.VMEM((16, WIDTH), jnp.float32),
            pltpu.VMEM((BODY, WIDTH), jnp.bfloat16),
            pltpu.SemaphoreType.DMA((10,)),
        ],
        compiler_params=pltpu.CompilerParams(vmem_limit_bytes=4 << 20),
        cost_estimate=pl.CostEstimate(flops=0, bytes_accessed=0, transcendentals=0),
        name="load",
    )(pltpu.with_memory_space_constraint(blocks.reshape(BODY, WIDTH), pltpu.HBM), kets)


def spread_kernel(tiles, counts, loads, dense, held, codes, listed, kets, sems):
    c, y, z = (lax.axis_index(a) for a in AXES[1:])
    sign = 1 - 2 * c
    rows, span = BODY + 16, SLOTS * WIDTH
    shards = loads.shape[0] // rows
    spare = dense.shape[0] // WIDTH - 1

    code_moves, block_moves = [], []
    for i in range(shards):
        code_moves.append(pltpu.make_async_copy(loads.at[pl.ds(i * rows + BODY, 16), :], codes.at[i], sems.at[i]))
        here = loads.at[pl.ds(i * rows + tiles[0] * span, len(tiles) * span), :]
        block_moves.append(pltpu.make_async_copy(here, held.at[i], sems.at[shards + i]))
    for move in code_moves + block_moves:
        move.start()

    def wipe(i, _):
        dense[pl.ds(pl.multiple_of(i * 512, 512), 512), :] = jnp.zeros((512, dense.shape[1]), dense.dtype)
        return 0

    lax.fori_loop(0, dense.shape[0] // 512, wipe, 0)
    for move in code_moves:
        move.wait()
    for i in range(shards):
        listed[i * 16:(i + 1) * 16, :] = codes[i].astype(jnp.float32).astype(jnp.int32)
    last = pltpu.make_async_copy(listed, kets, sems.at[2 * shards])
    last.start()
    last.wait()
    limits = [counts[t] for t in tiles]

    def place(i, n, j):
        k = kets[i * 16 + tiles[n], j]
        dz = (sign * (z - ((k >> 2) & 7))) & 7
        dy = y ^ (k >> 5)
        kind = jnp.where(dy == 0, 0, jnp.where(dy == 2, 3, jnp.where(dy == 1, 1 + c, 2 - c)))
        return jnp.where(i * SLOTS + j < limits[n], (dz * 4 + kind) * 4 + (k & 3), spare)

    for i in range(shards):
        block_moves[i].wait()

        def some(g, _, i=i):
            picks = [(n, g * 2 + d) for n in range(len(tiles)) for d in range(2)]
            spots = [place(i, n, j) for n, j in picks]
            blocks = [held[i, pl.ds(pl.multiple_of((n * SLOTS + j) * WIDTH, WIDTH), WIDTH), :] for n, j in picks]
            for (n, _), p, block in zip(picks, spots, blocks):
                dense[pl.ds(pl.multiple_of(p * WIDTH, WIDTH), WIDTH), n * WIDTH:(n + 1) * WIDTH] = block
            return 0

        lax.fori_loop(0, SLOTS // 2, some, 0, unroll=True)


def spread(counts, loads, tiles):
    shards = NX * NC
    return pl.pallas_call(
        functools.partial(spread_kernel, tiles),
        out_shape=pltpu.VMEM((NY * NZ * TILES * WIDTH + 512, len(tiles) * WIDTH), jnp.bfloat16),
        in_specs=[SMEM, pl.BlockSpec(memory_space=pltpu.HBM)],
        out_specs=VMEM,
        scratch_shapes=[
            pltpu.VMEM((shards, len(tiles) * SLOTS * WIDTH, WIDTH), jnp.bfloat16),
            pltpu.VMEM((shards, 16, WIDTH), jnp.bfloat16),
            pltpu.VMEM((shards * 16, WIDTH), jnp.int32),
            pltpu.SMEM((shards * 16, WIDTH), jnp.int32),
            pltpu.SemaphoreType.DMA((2 * shards + 1,)),
        ],
        compiler_params=pltpu.CompilerParams(vmem_limit_bytes=10 << 20),
        cost_estimate=pl.CostEstimate(flops=0, bytes_accessed=0, transcendentals=0),
        name="spread",
    )(counts, pltpu.with_memory_space_constraint(loads, pltpu.HBM))


def terms_kernel(places, fresh, *refs):
    dense, out = refs[:2], refs[-1]
    pieces = refs[2 if fresh else 3:-1]
    acc = None if fresh else refs[2][...]
    for piece, q in zip(pieces, places):
        left = jnp.concatenate([piece[t] for t in range(TILES)], axis=1)
        right = jnp.concatenate([d[q * 512:(q + 1) * 512, :] for d in dense], axis=1)
        part = jnp.dot(left, right, preferred_element_type=jnp.float32)
        acc = part if acc is None else acc + part
    out[...] = acc.astype(out.dtype)


def add_terms(dense, total, pieces, dtype=jnp.float32):
    rows = pieces[0][0].shape[1]
    fresh = total is None
    args = (dense[0], dense[1]) + (() if fresh else (total,)) + tuple(v for v, _ in pieces)
    return pl.pallas_call(
        functools.partial(terms_kernel, [q for _, q in pieces], fresh),
        out_shape=pltpu.VMEM((rows, TILES * WIDTH), dtype),
        in_specs=[VMEM] * len(args),
        out_specs=VMEM,
        compiler_params=pltpu.CompilerParams(vmem_limit_bytes=8 << 20),
        cost_estimate=pl.CostEstimate(flops=0, bytes_accessed=0, transcendentals=0),
        name="terms",
    )(*(near(v) for v in args))


def on_device(amplitudes, blocks, kets, counts):
    own = jnp.transpose(amplitudes, (1, 0, 2))
    load = make_load(blocks, kets)

    s, q, u, v = {0: own}, {}, {}, {}
    with jax.named_scope("loads"):
        everything = lax.all_gather(load, ("x", "core"), axis=0, tiled=True)
    order = Order()

    def along(a, k, name):
        a[k] = send(a[k - 1], ALONG_Z, name + str(k))

    def cross(a, b, k, name):
        b[k] = send(a[k], CROSS, name + str(k))

    def turn(k, more_s=(), more_u=(), more_q=(), more_v=()):
        order.meet((s, k), *more_s)
        if k + 1 < NZ:
            along(s, k + 1, "s")
        order.meet((u, k - 1), *more_u)
        cross(s, u, k, "u")
        order.meet((q, k - 1), *more_q)
        if k < NZ - 1:
            along(q, k, "q")
        order.meet((v, k - 2), *more_v)
        cross(q, v, k - 1, "v")

    along(s, 1, "s")
    q[0] = send(own, PARTNER, "q0")
    cross(s, u, 0, "u")
    s[7] = send(own, BACK_Z, "s7")
    order.meet((s, 1))
    along(s, 2, "s")
    cross(s, u, 1, "u")
    order.meet((q, 0))
    along(q, 1, "q")
    cross(q, v, 0, "v")
    order.meet((u, 0))
    order.meet((s, 7))
    for k in range(2, 6):
        turn(k)
    dense = {0: spread(counts, everything, (0, 1))}
    order.meet((s, 6), (dense, 0))
    cross(s, u, 6, "u")
    order.meet((u, 5))
    order.meet((q, 5))
    along(q, 6, "q")
    cross(q, v, 5, "v")
    dense[1] = spread(counts, everything, (2, 3))

    def terms(ks, names):
        return [(a[k], k * 4 + i) for k in ks for i, a in enumerate((s, q, u, v)) if "squv"[i] in names]

    total = {0: add_terms(dense, None, terms(range(0, 3), "squv"))}
    order.meet((v, 4), (u, 6), (total, 0), (s, 7), (v, 0), (q, 0))
    cross(s, u, 7, "u")
    q[7] = send(q[0], BACK_Z, "q7")
    v[7] = send(v[0], BACK_Z, "v7")
    order.meet((q, 6), (v, 5))
    cross(q, v, 6, "v")
    total[1] = add_terms(dense, total[0], terms((3,), "squv") + terms((4,), "squv") + terms((5,), "squ"))
    total = add_terms(dense, total[1], terms((5,), "v") + terms((6,), "squ") + terms((7,), "suv"))
    out = add_terms(dense, total, terms((7,), "q") + terms((6,), "v"), jnp.bfloat16)
    return out.reshape(out.shape[0], TILES, WIDTH)


def solution(mesh):
    grid = Mesh(mesh.devices.reshape(NX, NC, NY, NZ), AXES)
    placed = (
        P(("x", "core"), ("y", "z"), None),
        P(("y", "z"), ("x", "core"), None, None),
        P(("y", "z"), ("x", "core")),
        P(("y", "z")),
    )
    return jax.shard_map(
        on_device, mesh=grid, in_specs=placed, out_specs=P(("x", "core"), ("y", "z"), None), check_vma=False
    )
```
